32 devices in a mesh: row: 8 (over z, core), col: 4 (over y, x).
Axes of the slice: x: 2, y: 2, z: 4, core: 2. Of those that a mesh axis runs over, the one named last changes fastest.
Arguments:
- slab_block: bfloat16 [16384, 2048], P('row', 'col'), may hold values from -6 to 6
- scale_first: bfloat16 [16384], P('row'), may hold values from 0.5 to 2
- scale_second: bfloat16 [16384], P('row'), may hold values from 0.5 to 2
- panel_lower: bfloat16 [16384, 4096], P('row', 'col'), may hold values from -0.09375 to 0.09375
Outputs:
- updated_slab: bfloat16 [16384, 2048], P('row', 'col')
The draws below stay inside these ranges and needn't reach their ends.
All inputs are finite; a program needn't handle non-finite values.
Results may differ from the reference program's by a relative error of at most 0.015.
Values may be sent and summed in bfloat16 or wider, within the bound.
A program may use at most 64 MiB of HBM per device.

```python
import math
import jax
import jax.numpy as jnp
from jax import lax

SLAB_W = 2048
PANEL_W = 4096
ROWS_DEV = 2048
ORDER = 16384
N_ROW = 8
N_COL = 4


def level_of(own_key, shape, cuts, low, top_value):
    def one(position, blocks):
        steps = jax.random.uniform(jax.random.fold_in(jax.random.fold_in(own_key, 6), position), (blocks,), jnp.float32, low / len(cuts), top_value / len(cuts))
        return jnp.repeat(jnp.exp(steps), shape[position] // blocks).reshape((-1,) + (1,) * (len(shape) - position - 1))

    factor_of = one(*cuts[0])
    for cut in cuts[1:]:
        factor_of = factor_of * one(*cut)
    return factor_of


def normal_values(key, extent, scale, most, cuts=(), dtype=jnp.bfloat16):
    factor_of = level_of(key, extent, cuts, -0.22, 0.18) if cuts else 1.0
    values = jax.random.normal(key, extent, jnp.float32) * scale * factor_of
    return jnp.minimum(jnp.maximum(values, -most), most).astype(dtype)


def setup_inputs(seed: int = 0) -> dict:
    seeds = jax.random.split(jax.random.key(seed), 5)
    return {
        "slab_block": normal_values(seeds[0], (ORDER, SLAB_W), 1.0, 6.0, ((0, 8), (1, 4))),
        "scale_first": jnp.clip(jnp.exp(math.log(2.0) - 1.3862944 * jax.random.uniform(seeds[1], (ORDER,), jnp.float32) ** level_of(seeds[1], (ORDER,), ((0, 8),), -0.2, 0.2)), 0.5, 2.0).astype(jnp.bfloat16),
        "scale_second": jnp.clip(jnp.exp(math.log(2.0) - 1.3862944 * jax.random.uniform(seeds[2], (ORDER,), jnp.float32) ** level_of(seeds[2], (ORDER,), ((0, 8),), -0.2, 0.2)), 0.5, 2.0).astype(jnp.bfloat16),
        "panel_lower": normal_values(seeds[3], (ORDER, PANEL_W), PANEL_W ** -0.5, 0.09375, ((0, 8), (1, 4))),
    }


inv_root = 0.7071067811865476


def reference(slab_block, scale_first, scale_second, panel_lower):
    first = (scale_first.astype(jnp.float32)[:, None] * slab_block.astype(jnp.float32)).astype(jnp.bfloat16)
    first = lax.optimization_barrier(first).astype(jnp.float32)
    half_rows = ORDER // 2
    upper_half = first[:half_rows]
    lower_half = first[half_rows:]
    level_one = jnp.concatenate([(upper_half + lower_half) * inv_root, (upper_half - lower_half) * inv_root], axis=0)
    second = (scale_second.astype(jnp.float32)[:, None] * level_one).astype(jnp.bfloat16)
    second = lax.optimization_barrier(second).astype(jnp.float32)
    quads = second.reshape(2, 2, ORDER // 4, SLAB_W)
    level_two = jnp.stack([(quads[:, 0] + quads[:, 1]) * inv_root, (quads[:, 0] - quads[:, 1]) * inv_root], axis=1)
    transformed = level_two.reshape(ORDER, SLAB_W).astype(jnp.bfloat16)
    stored = transformed.reshape(ROWS_DEV, N_ROW, SLAB_W).transpose(1, 0, 2).reshape(ORDER, SLAB_W)
    upper_rows = transformed[:PANEL_W]
    block_width = PANEL_W // N_COL
    update_sum = jnp.zeros((ORDER, SLAB_W), jnp.float32)
    for blocknum in range(N_COL):
        term = jnp.dot(panel_lower[:, blocknum * block_width:(blocknum + 1) * block_width],
                       upper_rows[blocknum * block_width:(blocknum + 1) * block_width],
                       preferred_element_type=jnp.float32).astype(jnp.bfloat16)
        term = lax.optimization_barrier(term)
        update_sum = update_sum + term.astype(jnp.float32)
    return (stored.astype(jnp.float32) - update_sum).astype(jnp.bfloat16)
```

```python
import functools

import jax
import jax.numpy as jnp
from jax import lax
from jax.experimental import pallas as pl
from jax.experimental.pallas import tpu as pltpu
from jax.sharding import PartitionSpec as P

inv_root = 0.7071067811865476
F32, BF16 = jnp.float32, jnp.bfloat16


def column_of(row, size):
    a = lax.broadcasted_iota(jnp.int32, (size, size), 0)
    b = lax.broadcasted_iota(jnp.int32, (size, size), 1)
    return jnp.sum(jnp.where(a == b, row, 0.0), axis=1, keepdims=True)


def order_matrix(chunk, groups, natural_axis):
    per = chunk // groups
    natural = lax.broadcasted_iota(jnp.int32, (chunk, chunk), natural_axis)
    grouped = lax.broadcasted_iota(jnp.int32, (chunk, chunk), 1 - natural_axis)
    return jnp.where(natural == (grouped % per) * groups + grouped // per, 1.0, 0.0).astype(BF16)


def kernel(groups, cols, slab, s1, s2, panel, out, send, held, s2buf, tops, tops_nat, total, gath,
           own_sem, a2a_send, a2a_recv, s2_send, s2_recv, top_send, top_recv, fwd_send,
           pan_send, pan_recv):
    me, mc = lax.axis_index("row"), lax.axis_index("col")
    rows, width = slab.shape
    block = panel.shape[1]
    per_source = rows // groups
    top = cols * block // groups
    half = rows // 2
    chunk = max(256, 16 * groups)
    per = chunk // groups
    sibling = me + 1 - 2 * (me % 2)
    pairs = cols == 4
    col_x = mc + 1 - 2 * (mc % 2)
    col_y = mc + 2 - 4 * (mc // 2)

    def remote(src, dst, ssem, rsem, row=None, col=None):
        return pltpu.make_async_remote_copy(
            src_ref=src, dst_ref=dst, send_sem=ssem, recv_sem=rsem,
            device_id=(me if row is None else row, mc if col is None else col),
            device_id_type=pl.DeviceIdType.MESH)

    barrier = pltpu.get_barrier_semaphore()
    col_peers = [col_x, col_y] if pairs else [(mc + d) % cols for d in range(1, cols)]
    for d in range(1, groups):
        pl.semaphore_signal(barrier, inc=1, device_id=((me + d) % groups, mc),
                            device_id_type=pl.DeviceIdType.MESH)
    for peer in col_peers:
        pl.semaphore_signal(barrier, inc=1, device_id=(me, peer),
                            device_id_type=pl.DeviceIdType.MESH)
    own_panel = pltpu.make_async_copy(panel, gath.at[mc], own_sem.at[0])
    own_panel.start()
    pl.semaphore_wait(barrier, groups - 1 + len(col_peers))

    low, high = pl.ds(0, half), pl.ds(half, half)

    def panel_copy(n, part, peer, origin, src=None):
        source = panel.at[part] if src is None else src
        return remote(source, gath.at[origin, part], pan_send.at[n], pan_recv.at[n], col=peer)

    if pairs:
        panel_sends = [panel_copy(0, low, col_x, mc), panel_copy(1, high, col_y, mc),
                       panel_copy(2, high, col_x, mc), panel_copy(3, low, col_y, mc)]
    else:
        whole = pl.ds(0, rows)
        panel_sends = [panel_copy(d - 1, whole, (mc + d) % cols, mc) for d in range(1, cols)]
    for copy in panel_sends:
        copy.start()

    to_grouped = order_matrix(chunk, groups, 1)

    def scale_step(k, carry):
        scale = column_of(s1[pl.ds(k, 1), :], chunk)
        first = (scale * slab[pl.ds(k * chunk, chunk), :].astype(F32)).astype(BF16)
        moved = jnp.dot(to_grouped, first, preferred_element_type=F32).astype(BF16)
        for e in range(groups):
            send[e, pl.ds(k * per, per), :] = moved[e * per:(e + 1) * per]
        return carry

    lax.fori_loop(0, rows // chunk, scale_step, 0)
    place = pl.ds(me * per_source, per_source)
    exchange = []
    for d in range(1, groups):
        peer = (me + d) % groups
        exchange.append(remote(send.at[peer], held.at[place], a2a_send.at[d], a2a_recv.at[d],
                               row=peer))
        exchange.append(remote(s2, s2buf.at[me], s2_send.at[d], s2_recv.at[d], row=peer))
    for copy in exchange:
        copy.start()
    own_rows = pltpu.make_async_copy(send.at[me], held.at[place], own_sem.at[1])
    own_rows.start()
    own_scale = pltpu.make_async_copy(s2, s2buf.at[me], own_sem.at[2])
    own_scale.start()
    own_rows.wait()
    own_scale.wait()
    for d in range(1, groups):
        source = (me + groups - d) % groups
        remote(send.at[0], held.at[pl.ds(source * per_source, per_source)], a2a_send.at[d],
               a2a_recv.at[d], row=source).wait_recv()
        remote(s2, s2buf.at[source], s2_send.at[d], s2_recv.at[d], row=source).wait_recv()

    quarter = groups // 4

    def butterfly(u, carry):
        at = [pl.ds((u + n * quarter) * per_source, per_source) for n in range(4)]
        scale = [column_of(s2buf[u + n * quarter, pl.ds(me, 1), :], per_source) for n in range(4)]
        a = [held[at[n], :].astype(F32) for n in range(4)]
        one = [(a[0] + a[2]) * inv_root, (a[1] + a[3]) * inv_root,
               (a[0] - a[2]) * inv_root, (a[1] - a[3]) * inv_root]
        b = [(scale[n] * one[n]).astype(BF16).astype(F32) for n in range(4)]
        held[at[0], :] = ((b[0] + b[1]) * inv_root).astype(BF16)
        held[at[1], :] = ((b[0] - b[1]) * inv_root).astype(BF16)
        held[at[2], :] = ((b[2] + b[3]) * inv_root).astype(BF16)
        held[at[3], :] = ((b[2] - b[3]) * inv_root).astype(BF16)
        return carry

    lax.fori_loop(0, quarter, butterfly, 0)

    mine = held.at[pl.ds(0, top)]
    top_copies = []
    for d in range(2, groups, 2):
        top_copies.append(remote(mine, tops.at[me], top_send.at[d], top_recv.at[d],
                                 row=(me + d) % groups))
    top_copies.append(remote(mine, tops.at[me], top_send.at[0], top_recv.at[0], row=sibling))
    for copy in top_copies:
        copy.start()
    own_top = pltpu.make_async_copy(mine, tops.at[me], own_sem.at[3])
    own_top.start()

    if pairs:
        col_d = 3 - mc
        panel_sends[0].wait_recv()
        ahead = panel_copy(4, low, col_y, col_x, gath.at[col_x, low])
        ahead.start()
        panel_sends[1].wait_recv()
        across = panel_copy(5, high, col_x, col_y, gath.at[col_y, high])
        across.start()
        panel_sends += [ahead, across]

    forwards = []
    for d in range(2, groups, 2):
        source = (me + groups - d) % groups
        remote(mine, tops.at[source], top_send.at[d], top_recv.at[d], row=source).wait_recv()
        forward = remote(tops.at[source], tops.at[source], fwd_send.at[d], top_recv.at[d + 1],
                         row=sibling)
        forward.start()
        forwards.append(forward)
    own_top.wait()
    remote(mine, tops.at[sibling], top_send.at[0], top_recv.at[0], row=sibling).wait_recv()
    for d in range(2, groups, 2):
        source = (sibling + groups - d) % groups
        remote(tops.at[source], tops.at[source], fwd_send.at[d], top_recv.at[d + 1],
               row=sibling).wait_recv()

    to_natural = order_matrix(chunk, groups, 0)

    def natural_step(k, carry):
        pieces = [tops[e, pl.ds(k * per, per), :] for e in range(groups)]
        rows_now = jnp.dot(to_natural, jnp.concatenate(pieces, axis=0), preferred_element_type=F32)
        tops_nat[pl.ds(k * chunk, chunk), :] = rows_now.astype(BF16)
        return carry

    lax.fori_loop(0, cols * block // chunk, natural_step, 0)

    tile = 256

    def term(b, at):
        product = jnp.dot(gath[b, at, :], tops_nat[pl.ds(b * block, block), :],
                          preferred_element_type=F32)
        return product.astype(BF16).astype(F32)

    own_panel.wait()
    if pairs:
        panel_sends[2].wait_recv()
        panel_sends[3].wait_recv()

        def near_step(t, carry):
            at = pl.ds(t * tile, tile)
            total[at, :] = held[at, :].astype(F32) - (term(mc, at) + term(col_x, at) + term(col_y, at))
            return carry

        def far_step(t, carry):
            at = pl.ds(t * tile, tile)
            out[at, :] = (total[at, :] - term(col_d, at)).astype(BF16)
            return carry

        lax.fori_loop(0, rows // tile, near_step, 0)
        panel_copy(4, low, col_y, col_d, gath.at[col_d, low]).wait_recv()
        lax.fori_loop(0, half // tile, far_step, 0)
        panel_copy(5, high, col_x, col_d, gath.at[col_d, high]).wait_recv()
        lax.fori_loop(half // tile, rows // tile, far_step, 0)
    else:
        for copy in panel_sends:
            copy.wait_recv()

        def all_step(t, carry):
            at = pl.ds(t * tile, tile)

            def add(b, run):
                return run + term(b, at)

            update = lax.fori_loop(0, cols, add, jnp.zeros((tile, width), F32))
            out[at, :] = (held[at, :].astype(F32) - update).astype(BF16)
            return carry

        lax.fori_loop(0, rows // tile, all_step, 0)

    for copy in exchange + top_copies + forwards + panel_sends:
        copy.wait_send()


def per_device(slab_block, scale_first, scale_second, panel_lower):
    rows, width = slab_block.shape
    block = panel_lower.shape[1]
    groups, cols = lax.axis_size("row"), lax.axis_size("col")
    per_source = rows // groups
    top = cols * block // groups
    chunk = max(256, 16 * groups)
    s1 = scale_first.astype(F32).reshape(rows // chunk, chunk)
    s2 = scale_second.astype(F32).reshape(per_source, groups).T
    vmem = pl.BlockSpec(memory_space=pltpu.VMEM)
    dma = pltpu.SemaphoreType.DMA
    return pl.pallas_call(
        functools.partial(kernel, groups, cols),
        out_shape=jax.ShapeDtypeStruct((rows, width), BF16),
        in_specs=[vmem, vmem, vmem, pl.BlockSpec(memory_space=pl.ANY)],
        out_specs=vmem,
        scratch_shapes=[
            pltpu.VMEM((groups, per_source, width), BF16),
            pltpu.VMEM((rows, width), BF16),
            pltpu.VMEM((groups, groups, per_source), F32),
            pltpu.VMEM((groups, top, width), BF16),
            pltpu.VMEM((cols * block, width), BF16),
            pltpu.VMEM((rows, width), F32),
            pltpu.VMEM((cols, rows, block), BF16),
            dma((4,)),
            dma((groups,)), dma((groups,)), dma((groups,)), dma((groups,)),
            dma((groups,)), dma((groups,)), dma((groups,)),
            dma((max(6, cols),)), dma((max(6, cols),)),
        ],
        compiler_params=pltpu.CompilerParams(
            collective_id=0, has_side_effects=True, vmem_limit_bytes=56 * 2**20),
        cost_estimate=pl.CostEstimate(
            flops=2 * rows * cols * block * width,
            bytes_accessed=2 * (rows * width * 2 + rows * block), transcendentals=0),
    )(slab_block, s1, s2, panel_lower)


def solution(mesh):
    placed = (P("row", "col"), P("row"), P("row"), P("row", "col"))
    return jax.shard_map(
        per_device, mesh=mesh, in_specs=placed, out_specs=P("row", "col"), check_vma=False
    )
```

```python
import functools

import jax
import jax.numpy as jnp
from jax import lax
from jax.experimental import pallas as pl
from jax.experimental.pallas import tpu as pltpu
from jax.sharding import PartitionSpec as P

inv_root = 0.7071067811865476
F32, BF16 = jnp.float32, jnp.bfloat16


def column_of(row, size):
    a = lax.broadcasted_iota(jnp.int32, (size, size), 0)
    b = lax.broadcasted_iota(jnp.int32, (size, size), 1)
    return jnp.sum(jnp.where(a == b, row, 0.0), axis=1, keepdims=True)


def order_matrix(chunk, groups, natural_axis):
    per = chunk // groups
    natural = lax.broadcasted_iota(jnp.int32, (chunk, chunk), natural_axis)
    grouped = lax.broadcasted_iota(jnp.int32, (chunk, chunk), 1 - natural_axis)
    return jnp.where(natural == (grouped % per) * groups + grouped // per, 1.0, 0.0).astype(BF16)


def kernel(groups, cols, slab, s1, s2, panel, out, send, held, s2buf, tops, tops_nat, total, gath,
           own_sem, a2a_send, a2a_recv, s2_send, s2_recv, top_send, top_recv, fwd_send,
           pan_send, pan_recv):
    me, mc = lax.axis_index("row"), lax.axis_index("col")
    rows, width = slab.shape
    block = panel.shape[1]
    per_source = rows // groups
    top = cols * block // groups
    half = rows // 2
    chunk = max(256, 16 * groups)
    per = chunk // groups
    sibling = me + 1 - 2 * (me % 2)
    pairs = cols == 4
    col_x = mc + 1 - 2 * (mc % 2)
    col_y = mc + 2 - 4 * (mc // 2)

    def remote(src, dst, ssem, rsem, row=None, col=None):
        return pltpu.make_async_remote_copy(
            src_ref=src, dst_ref=dst, send_sem=ssem, recv_sem=rsem,
            device_id=(me if row is None else row, mc if col is None else col),
            device_id_type=pl.DeviceIdType.MESH)

    barrier = pltpu.get_barrier_semaphore()
    col_peers = [col_x, col_y] if pairs else [(mc + d) % cols for d in range(1, cols)]
    for d in range(1, groups):
        pl.semaphore_signal(barrier, inc=1, device_id=((me + d) % groups, mc),
                            device_id_type=pl.DeviceIdType.MESH)
    for peer in col_peers:
        pl.semaphore_signal(barrier, inc=1, device_id=(me, peer),
                            device_id_type=pl.DeviceIdType.MESH)
    own_panel = pltpu.make_async_copy(panel, gath.at[mc], own_sem.at[0])
    own_panel.start()
    pl.semaphore_wait(barrier, groups - 1 + len(col_peers))

    low, high = pl.ds(0, half), pl.ds(half, half)

    def panel_copy(n, part, peer, origin, src=None):
        source = panel.at[part] if src is None else src
        return remote(source, gath.at[origin, part], pan_send.at[n], pan_recv.at[n], col=peer)

    if pairs:
        panel_sends = [panel_copy(0, low, col_x, mc), panel_copy(1, high, col_y, mc),
                       panel_copy(2, high, col_x, mc), panel_copy(3, low, col_y, mc)]
    else:
        whole = pl.ds(0, rows)
        panel_sends = [panel_copy(d - 1, whole, (mc + d) % cols, mc) for d in range(1, cols)]
    for copy in panel_sends:
        copy.start()

    to_grouped = order_matrix(chunk, groups, 1)

    def scale_step(k, carry):
        scale = column_of(s1[pl.ds(k, 1), :], chunk)
        first = (scale * slab[pl.ds(k * chunk, chunk), :].astype(F32)).astype(BF16)
        moved = jnp.dot(to_grouped, first, preferred_element_type=F32).astype(BF16)
        for e in range(groups):
            send[e, pl.ds(k * per, per), :] = moved[e * per:(e + 1) * per]
        return carry

    lax.fori_loop(0, rows // chunk, scale_step, 0)
    place = pl.ds(me * per_source, per_source)
    exchange = []
    for d in range(1, groups):
        peer = (me + d) % groups
        exchange.append(remote(send.at[peer], held.at[place], a2a_send.at[d], a2a_recv.at[d],
                               row=peer))
        exchange.append(remote(s2, s2buf.at[me], s2_send.at[d], s2_recv.at[d], row=peer))
    for copy in exchange:
        copy.start()
    own_rows = pltpu.make_async_copy(send.at[me], held.at[place], own_sem.at[1])
    own_rows.start()
    own_scale = pltpu.make_async_copy(s2, s2buf.at[me], own_sem.at[2])
    own_scale.start()
    own_rows.wait()
    own_scale.wait()
    for d in range(1, groups):
        source = (me + groups - d) % groups
        remote(send.at[0], held.at[pl.ds(source * per_source, per_source)], a2a_send.at[d],
               a2a_recv.at[d], row=source).wait_recv()
        remote(s2, s2buf.at[source], s2_send.at[d], s2_recv.at[d], row=source).wait_recv()

    quarter = groups // 4

    def butterfly(u, carry):
        at = [pl.ds((u + n * quarter) * per_source, per_source) for n in range(4)]
        scale = [column_of(s2buf[u + n * quarter, pl.ds(me, 1), :], per_source) for n in range(4)]
        a = [held[at[n], :].astype(F32) for n in range(4)]
        one = [(a[0] + a[2]) * inv_root, (a[1] + a[3]) * inv_root,
               (a[0] - a[2]) * inv_root, (a[1] - a[3]) * inv_root]
        b = [(scale[n] * one[n]).astype(BF16).astype(F32) for n in range(4)]
        held[at[0], :] = ((b[0] + b[1]) * inv_root).astype(BF16)
        held[at[1], :] = ((b[0] - b[1]) * inv_root).astype(BF16)
        held[at[2], :] = ((b[2] + b[3]) * inv_root).astype(BF16)
        held[at[3], :] = ((b[2] - b[3]) * inv_root).astype(BF16)
        return carry

    lax.fori_loop(0, quarter, butterfly, 0)

    mine = held.at[pl.ds(0, top)]
    top_copies = []
    for d in range(2, groups, 2):
        top_copies.append(remote(mine, tops.at[me], top_send.at[d], top_recv.at[d],
                                 row=(me + d) % groups))
    top_copies.append(remote(mine, tops.at[me], top_send.at[0], top_recv.at[0], row=sibling))
    for copy in top_copies:
        copy.start()
    own_top = pltpu.make_async_copy(mine, tops.at[me], own_sem.at[3])
    own_top.start()

    if pairs:
        col_d = 3 - mc
        panel_sends[0].wait_recv()
        ahead = panel_copy(4, low, col_y, col_x, gath.at[col_x, low])
        ahead.start()
        panel_sends[1].wait_recv()
        across = panel_copy(5, high, col_x, col_y, gath.at[col_y, high])
        across.start()
        panel_sends += [ahead, across]

    forwards = []
    for d in range(2, groups, 2):
        source = (me + groups - d) % groups
        remote(mine, tops.at[source], top_send.at[d], top_recv.at[d], row=source).wait_recv()
        forward = remote(tops.at[source], tops.at[source], fwd_send.at[d], top_recv.at[d + 1],
                         row=sibling)
        forward.start()
        forwards.append(forward)
    own_top.wait()
    remote(mine, tops.at[sibling], top_send.at[0], top_recv.at[0], row=sibling).wait_recv()
    for d in range(2, groups, 2):
        source = (sibling + groups - d) % groups
        remote(tops.at[source], tops.at[source], fwd_send.at[d], top_recv.at[d + 1],
               row=sibling).wait_recv()

    to_natural = order_matrix(chunk, groups, 0)

    def natural_step(k, carry):
        pieces = [tops[e, pl.ds(k * per, per), :] for e in range(groups)]
        rows_now = jnp.dot(to_natural, jnp.concatenate(pieces, axis=0), preferred_element_type=F32)
        tops_nat[pl.ds(k * chunk, chunk), :] = rows_now.astype(BF16)
        return carry

    lax.fori_loop(0, cols * block // chunk, natural_step, 0)

    tile = 256

    def term(b, at):
        product = jnp.dot(gath[b, at, :], tops_nat[pl.ds(b * block, block), :],
                          preferred_element_type=F32)
        return product.astype(BF16).astype(F32)

    own_panel.wait()
    if pairs:
        panel_sends[2].wait_recv()
        panel_sends[3].wait_recv()

        def near_step(t, carry):
            at = pl.ds(t * tile, tile)
            total[at, :] = held[at, :].astype(F32) - (term(mc, at) + term(col_x, at) + term(col_y, at))
            return carry

        def far_step(t, carry):
            at = pl.ds(t * tile, tile)
            out[at, :] = (total[at, :] - term(col_d, at)).astype(BF16)
            return carry

        lax.fori_loop(0, rows // tile, near_step, 0)
        panel_copy(4, low, col_y, col_d, gath.at[col_d, low]).wait_recv()
        lax.fori_loop(0, half // tile, far_step, 0)
        panel_copy(5, high, col_x, col_d, gath.at[col_d, high]).wait_recv()
        lax.fori_loop(half // tile, rows // tile, far_step, 0)
    else:
        for copy in panel_sends:
            copy.wait_recv()

        def all_step(t, carry):
            at = pl.ds(t * tile, tile)

            def add(b, run):
                return run + term(b, at)

            update = lax.fori_loop(0, cols, add, jnp.zeros((tile, width), F32))
            out[at, :] = (held[at, :].astype(F32) - update).astype(BF16)
            return carry

        lax.fori_loop(0, rows // tile, all_step, 0)

    for copy in exchange + top_copies + forwards + panel_sends:
        copy.wait_send()


def paired_kernel(groups, parts, slab, scales, panel, out, send, held, s2buf, tops, tops_x, tops_y,
                  own, near_x, near_y, part_out, part_in, total,
                  own_sem, a2a_send, a2a_recv, s2_send, s2_recv, top_recv, chain_send, core_send,
                  x_send, x_recv, y_send, y_recv, xc_send, yc_send, sum_send, sum_recv,
                  pan_send, pan_recv):
    me, mc = lax.axis_index("row"), lax.axis_index("col")
    rows, _ = slab.shape
    width = held.shape[2]
    per_source = rows // groups
    half = rows // 2
    chunk = 256
    per = chunk // groups
    chips = groups // 2
    z, core = me // 2, me % 2
    y, x = mc // 2, mc % 2
    sibling = me + 1 - 2 * core
    col_x = mc + 1 - 2 * x
    col_y = mc + 2 - 4 * y
    block_rows = tops.shape[4]
    lines = rows // chunk
    s2 = scales.at[pl.ds(lines, lines)]

    def remote(src, dst, ssem, rsem, row=None, col=None):
        return pltpu.make_async_remote_copy(
            src_ref=src, dst_ref=dst, send_sem=ssem, recv_sem=rsem,
            device_id=(me if row is None else row, mc if col is None else col),
            device_id_type=pl.DeviceIdType.MESH)

    barrier = pltpu.get_barrier_semaphore()
    for d in range(1, groups):
        pl.semaphore_signal(barrier, inc=1, device_id=((me + d) % groups, mc),
                            device_id_type=pl.DeviceIdType.MESH)
    for peer in (col_x, col_y):
        pl.semaphore_signal(barrier, inc=1, device_id=(me, peer),
                            device_id_type=pl.DeviceIdType.MESH)
    own_panel = pltpu.make_async_copy(panel, own, own_sem.at[0])
    own_panel.start()
    pl.semaphore_wait(barrier, groups + 1)

    panel_x = remote(panel.at[pl.ds(0, half)], near_x, pan_send.at[0], pan_recv.at[0], col=col_x)
    panel_y = remote(panel.at[pl.ds(half, half)], near_y, pan_send.at[1], pan_recv.at[1], col=col_y)
    panel_x.start()
    panel_y.start()

    to_grouped = order_matrix(chunk, groups, 1)
    place = pl.ds(me * per_source, per_source)

    def scaled(q):
        def step(k, carry):
            scale = column_of(scales[pl.ds(k, 1), :], chunk)
            lanes = slice(q * width, (q + 1) * width)
            first = (scale * slab[pl.ds(k * chunk, chunk), lanes].astype(F32)).astype(BF16)
            moved = jnp.dot(to_grouped, first, preferred_element_type=F32).astype(BF16)
            for e in range(groups):
                send[q, e, pl.ds(k * per, per), :] = moved[e * per:(e + 1) * per]
            return carry

        lax.fori_loop(0, rows // chunk, step, 0)

    def exchange(q):
        for d in range(1, groups):
            peer = (me + d) % groups
            copy = remote(send.at[q, peer], held.at[q, place], a2a_send.at[q, d],
                          a2a_recv.at[q, d], row=peer)
            copy.start()
            sends.append(copy)

    sends = []
    for d in range(1, groups):
        peer = (me + d) % groups
        copy = remote(s2, s2buf.at[me], s2_send.at[d], s2_recv.at[d], row=peer)
        copy.start()
        sends.append(copy)
    scaled(0)
    exchange(0)
    for q in range(1, parts):
        scaled(q)
    own_copies = [pltpu.make_async_copy(s2, s2buf.at[me], own_sem.at[1])]
    for q in range(parts):
        own_copies.append(pltpu.make_async_copy(send.at[q, me], held.at[q, place],
                                                own_sem.at[2 + q]))
    for copy in own_copies:
        copy.start()

    to_columns = order_matrix(chunk, groups, 0)

    def regroup(ref):
        def step(t, carry):
            at = pl.ds(t * chunk, chunk)
            for n in range(ref.shape[1] // chunk):
                lanes = slice(n * chunk, (n + 1) * chunk)
                ref[at, lanes] = jnp.dot(ref[at, lanes], to_columns,
                                         preferred_element_type=F32).astype(BF16)
            return carry

        lax.fori_loop(0, ref.shape[0] // chunk, step, 0)

    own_panel.wait()
    regroup(own)
    for copy in own_copies:
        copy.wait()
    for d in range(1, groups):
        source = (me + groups - d) % groups
        remote(s2, s2buf.at[source], s2_send.at[d], s2_recv.at[d], row=source).wait_recv()

    quarter = groups // 4

    def top_rows(q):
        for d in range(1, groups):
            source = (me + groups - d) % groups
            remote(send.at[q, 0], held.at[q, pl.ds(source * per_source, per_source)],
                   a2a_send.at[q, d], a2a_recv.at[q, d], row=source).wait_recv()

        def step(u, carry):
            a = [held[q, source_rows(u, n), :].astype(F32) for n in range(4)]
            one = [(a[0] + a[2]) * inv_root, (a[1] + a[3]) * inv_root]
            b = [(second_scale(u + n * quarter) * one[n]).astype(BF16).astype(F32)
                 for n in range(2)]
            upper = ((b[0] + b[1]) * inv_root).astype(BF16)
            tops[q, me, u, 0] = upper[:block_rows]
            tops[q, me, u, 1] = upper[block_rows:]
            return carry

        lax.fori_loop(0, quarter, step, 0)

    def source_rows(u, n):
        return pl.ds((u + n * quarter) * per_source, per_source)

    def second_scale(source):
        j = lax.broadcasted_iota(jnp.int32, (per, chunk), 0)
        natural = lax.broadcasted_iota(jnp.int32, (per, chunk), 1)
        here = natural == j * groups + me
        return jnp.concatenate(
            [jnp.sum(jnp.where(here, s2buf[source, k:k + 1, :], 0.0), axis=1, keepdims=True)
             for k in range(lines)], axis=0)

    def all_rows(q):
        def step(u, carry):
            at = [source_rows(u, n) for n in range(4)]
            a = [held[q, at[n], :].astype(F32) for n in range(4)]
            one = [(a[0] + a[2]) * inv_root, (a[1] + a[3]) * inv_root,
                   (a[0] - a[2]) * inv_root, (a[1] - a[3]) * inv_root]
            b = [(second_scale(u + n * quarter) * one[n]).astype(BF16).astype(F32)
                 for n in range(4)]
            held[q, at[0], :] = ((b[0] + b[1]) * inv_root).astype(BF16)
            held[q, at[1], :] = ((b[0] - b[1]) * inv_root).astype(BF16)
            held[q, at[2], :] = ((b[2] + b[3]) * inv_root).astype(BF16)
            held[q, at[3], :] = ((b[2] - b[3]) * inv_root).astype(BF16)
            return carry

        lax.fori_loop(0, quarter, step, 0)

    def chain(q, chip, way):
        e = 2 * chip + core
        to = (me + 2) % groups if way == 0 else (me + groups - 2) % groups
        return remote(tops.at[q, e], tops.at[q, e], chain_send.at[q, way, chip],
                      top_recv.at[q, e], row=to)

    def to_core(q, e):
        return remote(tops.at[q, e], tops.at[q, e], core_send.at[q, e], top_recv.at[q, e],
                      row=sibling)

    def to_x(q, e):
        return remote(tops.at[q, e, :, 1 - x], tops_x.at[q, e], x_send.at[q, e], x_recv.at[q, e],
                      col=col_x)

    def to_y(q, e):
        return remote(tops.at[q, e, 1 - y], tops_y.at[q, e], y_send.at[q, e], y_recv.at[q, e],
                      col=col_y)

    def x_core(q, e):
        return remote(tops_x.at[q, e], tops_x.at[q, e], xc_send.at[q, e], x_recv.at[q, e],
                      row=sibling)

    def y_core(q, e):
        return remote(tops_y.at[q, e], tops_y.at[q, e], yc_send.at[q, e], y_recv.at[q, e],
                      row=sibling)

    def spread(q, chip):
        e = 2 * chip + core
        to_x(q, e).start()
        to_y(q, e).start()
        to_core(q, e).start()

    def begin(q):
        @pl.when(z + 1 < chips)
        def _():
            chain(q, z, 0).start()

        @pl.when(z > 0)
        def _():
            chain(q, z, 1).start()

        spread(q, z)

    def onward(q, k):
        @pl.when(z >= k)
        def _():
            chain(q, z - k, 0).wait_recv()

            @pl.when(z + 1 < chips)
            def _():
                chain(q, z - k, 0).start()

            spread(q, z - k)

        @pl.when(z + k < chips)
        def _():
            chain(q, z + k, 1).wait_recv()

            @pl.when(z > 0)
            def _():
                chain(q, z + k, 1).start()

            spread(q, z + k)

    def collect(q):
        for chip in range(chips):
            e = 2 * chip + core
            to_x(q, e).wait_recv()
            x_core(q, e).start()
            to_y(q, e).wait_recv()
            y_core(q, e).start()
        for chip in range(chips):
            other = 2 * chip + 1 - core
            to_core(q, other).wait_recv()
            x_core(q, other).wait_recv()
            y_core(q, other).wait_recv()

    pieces = [(e, slice(n * per, (n + 1) * per))
              for n in range(block_rows // per) for e in range(groups)]

    def own_top(q, by, bx):
        return jnp.concatenate([tops[q, e, by, bx, at, :] for e, at in pieces], axis=0)

    def far_top(ref, q, b):
        return jnp.concatenate([ref[q, e, b, at, :] for e, at in pieces], axis=0)

    tile = 256
    tiles = half // tile

    def product(a, b):
        return jnp.dot(a, b, preferred_element_type=F32)

    def sum_copy(q, t, high):
        at = pl.ds(t * tile + (half if high else 0), tile)
        n = t + (tiles if high else 0)
        return remote(part_out.at[q, at], part_in.at[q, at], sum_send.at[q, n], sum_recv.at[q, n],
                      col=col_x if high else col_y)

    def send_sums(q):
        def step(t, carry):
            at, upper = pl.ds(t * tile, tile), pl.ds(half + t * tile, tile)
            part_out[q, at, :] = (product(own[at, :], far_top(tops_y, q, x)) +
                                  product(near_x[at, :], far_top(tops_y, q, 1 - x))).astype(BF16)
            sum_copy(q, t, False).start()
            part_out[q, upper, :] = (product(own[upper, :], far_top(tops_x, q, y)) +
                                     product(near_y[at, :], far_top(tops_x, q, 1 - y))
                                     ).astype(BF16)
            sum_copy(q, t, True).start()
            return carry

        lax.fori_loop(0, tiles, step, 0)

    def own_sums(q):
        def step(t, carry):
            at, upper = pl.ds(t * tile, tile), pl.ds(half + t * tile, tile)
            mine = own_top(q, y, x)
            total[q, at, :] = held[q, at, :].astype(F32) - (
                product(own[at, :], mine) + product(near_x[at, :], own_top(q, y, 1 - x)))
            total[q, upper, :] = held[q, upper, :].astype(F32) - (
                product(own[upper, :], mine) + product(near_y[at, :], own_top(q, 1 - y, x)))
            return carry

        lax.fori_loop(0, tiles, step, 0)

    def finish(q):
        lanes = slice(q * width, (q + 1) * width)

        def step(t, carry):
            for high in (False, True):
                sum_copy(q, t, high).wait_recv()
                at = pl.ds(t * tile + (half if high else 0), tile)
                out[at, lanes] = (total[q, at, :] - part_in[q, at, :].astype(F32)).astype(BF16)
            return carry

        lax.fori_loop(0, tiles, step, 0)

    top_rows(0)
    begin(0)
    exchange(1)
    all_rows(0)
    onward(0, 1)
    panel_x.wait_recv()
    panel_y.wait_recv()
    regroup(near_x)
    regroup(near_y)
    onward(0, 2)
    top_rows(1)
    begin(1)
    all_rows(1)
    onward(0, 3)
    onward(1, 1)
    collect(0)
    onward(1, 2)
    send_sums(0)
    onward(1, 3)
    own_sums(0)
    collect(1)
    send_sums(1)
    own_sums(1)
    finish(0)
    finish(1)

    for copy in sends + [panel_x, panel_y]:
        copy.wait_send()
    for q in range(parts):
        for chip in range(chips):
            @pl.when((z + 1 < chips) & (chip <= z))
            def _():
                chain(q, chip, 0).wait_send()

            @pl.when((z > 0) & (chip >= z))
            def _():
                chain(q, chip, 1).wait_send()

            e = 2 * chip + core
            for copy in (to_x(q, e), to_y(q, e), to_core(q, e), x_core(q, e), y_core(q, e)):
                copy.wait_send()

        def done(t, carry):
            sum_copy(q, t, False).wait_send()
            sum_copy(q, t, True).wait_send()
            return carry

        lax.fori_loop(0, tiles, done, 0)


def paired_scratch(groups, parts, rows, block, width):
    dma = pltpu.SemaphoreType.DMA
    piece, upper = width // parts, block // groups
    pair = dma((parts, groups))
    return [
        pltpu.VMEM((parts, groups, rows // groups, piece), BF16),
        pltpu.VMEM((parts, rows, piece), BF16),
        pltpu.VMEM((groups, rows // 256, 256), F32),
        pltpu.VMEM((parts, groups, 2, 2, upper, piece), BF16),
        pltpu.VMEM((parts, groups, 2, upper, piece), BF16),
        pltpu.VMEM((parts, groups, 2, upper, piece), BF16),
        pltpu.VMEM((rows, block), BF16),
        pltpu.VMEM((rows // 2, block), BF16),
        pltpu.VMEM((rows // 2, block), BF16),
        pltpu.VMEM((parts, rows, piece), BF16),
        pltpu.VMEM((parts, rows, piece), BF16),
        pltpu.VMEM((parts, rows, piece), F32),
        dma((2 + parts,)), pair, pair, dma((groups,)), dma((groups,)), pair,
        dma((parts, 2, groups // 2)), pair,
        pair, pair, pair, pair, pair, pair,
        dma((parts, rows // 256)), dma((parts, rows // 256)), dma((2,)), dma((2,)),
    ]


def per_device(slab_block, scale_first, scale_second, panel_lower):
    rows, width = slab_block.shape
    block = panel_lower.shape[1]
    groups, cols = lax.axis_size("row"), lax.axis_size("col")
    per_source = rows // groups
    top = cols * block // groups
    chunk = max(256, 16 * groups)
    vmem = pl.BlockSpec(memory_space=pltpu.VMEM)
    dma = pltpu.SemaphoreType.DMA
    if groups == 8 and cols == 4 and rows == 2 * block and width % 256 == 0:
        parts = 2
        run = functools.partial(paired_kernel, groups, parts)
        both = jnp.concatenate([scale_first, scale_second]).astype(F32)
        scales = [both.reshape(2 * rows // chunk, chunk)]
        scratch = paired_scratch(groups, parts, rows, block, width)
    else:
        run = functools.partial(kernel, groups, cols)
        scales = [scale_first.astype(F32).reshape(rows // chunk, chunk),
                  scale_second.astype(F32).reshape(per_source, groups).T]
        scratch = [
            pltpu.VMEM((groups, per_source, width), BF16),
            pltpu.VMEM((rows, width), BF16),
            pltpu.VMEM((groups, groups, per_source), F32),
            pltpu.VMEM((groups, top, width), BF16),
            pltpu.VMEM((cols * block, width), BF16),
            pltpu.VMEM((rows, width), F32),
            pltpu.VMEM((cols, rows, block), BF16),
            dma((4,)),
            dma((groups,)), dma((groups,)), dma((groups,)), dma((groups,)),
            dma((groups,)), dma((groups,)), dma((groups,)),
            dma((max(6, cols),)), dma((max(6, cols),)),
        ]
    return pl.pallas_call(
        run,
        out_shape=jax.ShapeDtypeStruct((rows, width), BF16),
        in_specs=[vmem] * (1 + len(scales)) + [pl.BlockSpec(memory_space=pl.ANY)],
        out_specs=vmem,
        scratch_shapes=scratch,
        compiler_params=pltpu.CompilerParams(
            collective_id=0, has_side_effects=True, vmem_limit_bytes=56 * 2**20),
        cost_estimate=pl.CostEstimate(
            flops=2 * rows * cols * block * width,
            bytes_accessed=2 * (rows * width * 2 + rows * block), transcendentals=0),
    )(slab_block, *scales, panel_lower)


def solution(mesh):
    placed = (P("row", "col"), P("row"), P("row"), P("row", "col"))
    return jax.shard_map(
        per_device, mesh=mesh, in_specs=placed, out_specs=P("row", "col"), check_vma=False
    )
```

```python
import functools

import jax
import jax.numpy as jnp
from jax import lax
from jax.experimental import pallas as pl
from jax.experimental.pallas import tpu as pltpu
from jax.sharding import PartitionSpec as P

inv_root = 0.7071067811865476
F32, BF16 = jnp.float32, jnp.bfloat16


def column_of(row, size):
    a = lax.broadcasted_iota(jnp.int32, (size, size), 0)
    b = lax.broadcasted_iota(jnp.int32, (size, size), 1)
    return jnp.sum(jnp.where(a == b, row, 0.0), axis=1, keepdims=True)


def order_matrix(chunk, groups, natural_axis):
    per = chunk // groups
    natural = lax.broadcasted_iota(jnp.int32, (chunk, chunk), natural_axis)
    grouped = lax.broadcasted_iota(jnp.int32, (chunk, chunk), 1 - natural_axis)
    return jnp.where(natural == (grouped % per) * groups + grouped // per, 1.0, 0.0).astype(BF16)


def kernel(groups, cols, slab, s1, s2, panel, out, send, held, s2buf, tops, tops_nat, total, gath,
           own_sem, a2a_send, a2a_recv, s2_send, s2_recv, top_send, top_recv, fwd_send,
           pan_send, pan_recv):
    me, mc = lax.axis_index("row"), lax.axis_index("col")
    rows, width = slab.shape
    block = panel.shape[1]
    per_source = rows // groups
    top = cols * block // groups
    half = rows // 2
    chunk = max(256, 16 * groups)
    per = chunk // groups
    sibling = me + 1 - 2 * (me % 2)
    pairs = cols == 4
    col_x = mc + 1 - 2 * (mc % 2)
    col_y = mc + 2 - 4 * (mc // 2)

    def remote(src, dst, ssem, rsem, row=None, col=None):
        return pltpu.make_async_remote_copy(
            src_ref=src, dst_ref=dst, send_sem=ssem, recv_sem=rsem,
            device_id=(me if row is None else row, mc if col is None else col),
            device_id_type=pl.DeviceIdType.MESH)

    barrier = pltpu.get_barrier_semaphore()
    col_peers = [col_x, col_y] if pairs else [(mc + d) % cols for d in range(1, cols)]
    for d in range(1, groups):
        pl.semaphore_signal(barrier, inc=1, device_id=((me + d) % groups, mc),
                            device_id_type=pl.DeviceIdType.MESH)
    for peer in col_peers:
        pl.semaphore_signal(barrier, inc=1, device_id=(me, peer),
                            device_id_type=pl.DeviceIdType.MESH)
    own_panel = pltpu.make_async_copy(panel, gath.at[mc], own_sem.at[0])
    own_panel.start()
    pl.semaphore_wait(barrier, groups - 1 + len(col_peers))

    low, high = pl.ds(0, half), pl.ds(half, half)

    def panel_copy(n, part, peer, origin, src=None):
        source = panel.at[part] if src is None else src
        return remote(source, gath.at[origin, part], pan_send.at[n], pan_recv.at[n], col=peer)

    if pairs:
        panel_sends = [panel_copy(0, low, col_x, mc), panel_copy(1, high, col_y, mc),
                       panel_copy(2, high, col_x, mc), panel_copy(3, low, col_y, mc)]
    else:
        whole = pl.ds(0, rows)
        panel_sends = [panel_copy(d - 1, whole, (mc + d) % cols, mc) for d in range(1, cols)]
    for copy in panel_sends:
        copy.start()

    to_grouped = order_matrix(chunk, groups, 1)

    def scale_step(k, carry):
        scale = column_of(s1[pl.ds(k, 1), :], chunk)
        first = (scale * slab[pl.ds(k * chunk, chunk), :].astype(F32)).astype(BF16)
        moved = jnp.dot(to_grouped, first, preferred_element_type=F32).astype(BF16)
        for e in range(groups):
            send[e, pl.ds(k * per, per), :] = moved[e * per:(e + 1) * per]
        return carry

    lax.fori_loop(0, rows // chunk, scale_step, 0)
    place = pl.ds(me * per_source, per_source)
    exchange = []
    for d in range(1, groups):
        peer = (me + d) % groups
        exchange.append(remote(send.at[peer], held.at[place], a2a_send.at[d], a2a_recv.at[d],
                               row=peer))
        exchange.append(remote(s2, s2buf.at[me], s2_send.at[d], s2_recv.at[d], row=peer))
    for copy in exchange:
        copy.start()
    own_rows = pltpu.make_async_copy(send.at[me], held.at[place], own_sem.at[1])
    own_rows.start()
    own_scale = pltpu.make_async_copy(s2, s2buf.at[me], own_sem.at[2])
    own_scale.start()
    own_rows.wait()
    own_scale.wait()
    for d in range(1, groups):
        source = (me + groups - d) % groups
        remote(send.at[0], held.at[pl.ds(source * per_source, per_source)], a2a_send.at[d],
               a2a_recv.at[d], row=source).wait_recv()
        remote(s2, s2buf.at[source], s2_send.at[d], s2_recv.at[d], row=source).wait_recv()

    quarter = groups // 4

    def butterfly(u, carry):
        at = [pl.ds((u + n * quarter) * per_source, per_source) for n in range(4)]
        scale = [column_of(s2buf[u + n * quarter, pl.ds(me, 1), :], per_source) for n in range(4)]
        a = [held[at[n], :].astype(F32) for n in range(4)]
        one = [(a[0] + a[2]) * inv_root, (a[1] + a[3]) * inv_root,
               (a[0] - a[2]) * inv_root, (a[1] - a[3]) * inv_root]
        b = [(scale[n] * one[n]).astype(BF16).astype(F32) for n in range(4)]
        held[at[0], :] = ((b[0] + b[1]) * inv_root).astype(BF16)
        held[at[1], :] = ((b[0] - b[1]) * inv_root).astype(BF16)
        held[at[2], :] = ((b[2] + b[3]) * inv_root).astype(BF16)
        held[at[3], :] = ((b[2] - b[3]) * inv_root).astype(BF16)
        return carry

    lax.fori_loop(0, quarter, butterfly, 0)

    mine = held.at[pl.ds(0, top)]
    top_copies = []
    for d in range(2, groups, 2):
        top_copies.append(remote(mine, tops.at[me], top_send.at[d], top_recv.at[d],
                                 row=(me + d) % groups))
    top_copies.append(remote(mine, tops.at[me], top_send.at[0], top_recv.at[0], row=sibling))
    for copy in top_copies:
        copy.start()
    own_top = pltpu.make_async_copy(mine, tops.at[me], own_sem.at[3])
    own_top.start()

    if pairs:
        col_d = 3 - mc
        panel_sends[0].wait_recv()
        ahead = panel_copy(4, low, col_y, col_x, gath.at[col_x, low])
        ahead.start()
        panel_sends[1].wait_recv()
        across = panel_copy(5, high, col_x, col_y, gath.at[col_y, high])
        across.start()
        panel_sends += [ahead, across]

    forwards = []
    for d in range(2, groups, 2):
        source = (me + groups - d) % groups
        remote(mine, tops.at[source], top_send.at[d], top_recv.at[d], row=source).wait_recv()
        forward = remote(tops.at[source], tops.at[source], fwd_send.at[d], top_recv.at[d + 1],
                         row=sibling)
        forward.start()
        forwards.append(forward)
    own_top.wait()
    remote(mine, tops.at[sibling], top_send.at[0], top_recv.at[0], row=sibling).wait_recv()
    for d in range(2, groups, 2):
        source = (sibling + groups - d) % groups
        remote(tops.at[source], tops.at[source], fwd_send.at[d], top_recv.at[d + 1],
               row=sibling).wait_recv()

    to_natural = order_matrix(chunk, groups, 0)

    def natural_step(k, carry):
        pieces = [tops[e, pl.ds(k * per, per), :] for e in range(groups)]
        rows_now = jnp.dot(to_natural, jnp.concatenate(pieces, axis=0), preferred_element_type=F32)
        tops_nat[pl.ds(k * chunk, chunk), :] = rows_now.astype(BF16)
        return carry

    lax.fori_loop(0, cols * block // chunk, natural_step, 0)

    tile = 256

    def term(b, at):
        product = jnp.dot(gath[b, at, :], tops_nat[pl.ds(b * block, block), :],
                          preferred_element_type=F32)
        return product.astype(BF16).astype(F32)

    own_panel.wait()
    if pairs:
        panel_sends[2].wait_recv()
        panel_sends[3].wait_recv()

        def near_step(t, carry):
            at = pl.ds(t * tile, tile)
            total[at, :] = held[at, :].astype(F32) - (term(mc, at) + term(col_x, at) + term(col_y, at))
            return carry

        def far_step(t, carry):
            at = pl.ds(t * tile, tile)
            out[at, :] = (total[at, :] - term(col_d, at)).astype(BF16)
            return carry

        lax.fori_loop(0, rows // tile, near_step, 0)
        panel_copy(4, low, col_y, col_d, gath.at[col_d, low]).wait_recv()
        lax.fori_loop(0, half // tile, far_step, 0)
        panel_copy(5, high, col_x, col_d, gath.at[col_d, high]).wait_recv()
        lax.fori_loop(half // tile, rows // tile, far_step, 0)
    else:
        for copy in panel_sends:
            copy.wait_recv()

        def all_step(t, carry):
            at = pl.ds(t * tile, tile)

            def add(b, run):
                return run + term(b, at)

            update = lax.fori_loop(0, cols, add, jnp.zeros((tile, width), F32))
            out[at, :] = (held[at, :].astype(F32) - update).astype(BF16)
            return carry

        lax.fori_loop(0, rows // tile, all_step, 0)

    for copy in exchange + top_copies + forwards + panel_sends:
        copy.wait_send()


def paired_kernel(groups, parts, slab, scales, panel, out, send, held, s2buf, tops, tops_x, tops_y,
                  own, near_x, near_y, part_out, part_in, total,
                  own_sem, a2a_send, a2a_recv, s2_send, s2_recv, top_recv, chain_send, core_send,
                  x_send, x_recv, y_send, y_recv, xc_send, yc_send, sum_send, sum_recv,
                  pan_send, pan_recv):
    me, mc = lax.axis_index("row"), lax.axis_index("col")
    rows, _ = slab.shape
    width = held.shape[2]
    per_source = rows // groups
    half = rows // 2
    chunk = 256
    per = chunk // groups
    chips = groups // 2
    z, core = me // 2, me % 2
    y, x = mc // 2, mc % 2
    sibling = me + 1 - 2 * core
    col_x = mc + 1 - 2 * x
    col_y = mc + 2 - 4 * y
    block_rows = tops.shape[4]
    lines = rows // chunk
    s2 = scales.at[pl.ds(lines, lines)]

    def remote(src, dst, ssem, rsem, row=None, col=None):
        return pltpu.make_async_remote_copy(
            src_ref=src, dst_ref=dst, send_sem=ssem, recv_sem=rsem,
            device_id=(me if row is None else row, mc if col is None else col),
            device_id_type=pl.DeviceIdType.MESH)

    barrier = pltpu.get_barrier_semaphore()
    for d in range(1, groups):
        pl.semaphore_signal(barrier, inc=1, device_id=((me + d) % groups, mc),
                            device_id_type=pl.DeviceIdType.MESH)
    for peer in (col_x, col_y):
        pl.semaphore_signal(barrier, inc=1, device_id=(me, peer),
                            device_id_type=pl.DeviceIdType.MESH)
    own_panel = pltpu.make_async_copy(panel, own, own_sem.at[0])
    own_panel.start()
    pl.semaphore_wait(barrier, groups + 1)

    panel_x = remote(panel.at[pl.ds(0, half)], near_x, pan_send.at[0], pan_recv.at[0], col=col_x)
    panel_y = remote(panel.at[pl.ds(half, half)], near_y, pan_send.at[1], pan_recv.at[1], col=col_y)
    panel_x.start()
    panel_y.start()

    to_grouped = order_matrix(chunk, groups, 1)
    place = pl.ds(me * per_source, per_source)

    def scaled(q):
        def step(k, carry):
            scale = column_of(scales[pl.ds(k, 1), :], chunk)
            lanes = slice(q * width, (q + 1) * width)
            first = (scale * slab[pl.ds(k * chunk, chunk), lanes].astype(F32)).astype(BF16)
            moved = jnp.dot(to_grouped, first, preferred_element_type=F32).astype(BF16)
            for e in range(groups):
                send[q, e, pl.ds(k * per, per), :] = moved[e * per:(e + 1) * per]
            return carry

        lax.fori_loop(0, rows // chunk, step, 0)

    def exchange(q):
        for d in range(1, groups):
            peer = (me + d) % groups
            copy = remote(send.at[q, peer], held.at[q, place], a2a_send.at[q, d],
                          a2a_recv.at[q, d], row=peer)
            copy.start()
            sends.append(copy)

    sends = []
    for d in range(1, groups):
        peer = (me + d) % groups
        copy = remote(s2, s2buf.at[me], s2_send.at[d], s2_recv.at[d], row=peer)
        copy.start()
        sends.append(copy)
    scaled(0)
    exchange(0)
    for q in range(1, parts):
        scaled(q)
    own_copies = [pltpu.make_async_copy(s2, s2buf.at[me], own_sem.at[1])]
    for q in range(parts):
        own_copies.append(pltpu.make_async_copy(send.at[q, me], held.at[q, place],
                                                own_sem.at[2 + q]))
    for copy in own_copies:
        copy.start()

    to_columns = order_matrix(chunk, groups, 0)

    def regroup(ref):
        def step(t, carry):
            at = pl.ds(t * chunk, chunk)
            for n in range(ref.shape[1] // chunk):
                lanes = slice(n * chunk, (n + 1) * chunk)
                ref[at, lanes] = jnp.dot(ref[at, lanes], to_columns,
                                         preferred_element_type=F32).astype(BF16)
            return carry

        lax.fori_loop(0, ref.shape[0] // chunk, step, 0)

    own_panel.wait()
    regroup(own)
    for copy in own_copies:
        copy.wait()
    for d in range(1, groups):
        source = (me + groups - d) % groups
        remote(s2, s2buf.at[source], s2_send.at[d], s2_recv.at[d], row=source).wait_recv()

    quarter = groups // 4

    def top_rows(q):
        for d in range(1, groups):
            source = (me + groups - d) % groups
            remote(send.at[q, 0], held.at[q, pl.ds(source * per_source, per_source)],
                   a2a_send.at[q, d], a2a_recv.at[q, d], row=source).wait_recv()

        def step(u, carry):
            a = [held[q, source_rows(u, n), :].astype(F32) for n in range(4)]
            one = [(a[0] + a[2]) * inv_root, (a[1] + a[3]) * inv_root]
            b = [(second_scale(u + n * quarter) * one[n]).astype(BF16).astype(F32)
                 for n in range(2)]
            upper = ((b[0] + b[1]) * inv_root).astype(BF16)
            tops[q, me, u, 0] = upper[:block_rows]
            tops[q, me, u, 1] = upper[block_rows:]
            return carry

        lax.fori_loop(0, quarter, step, 0)

    def source_rows(u, n):
        return pl.ds((u + n * quarter) * per_source, per_source)

    def second_scale(source):
        j = lax.broadcasted_iota(jnp.int32, (per, chunk), 0)
        natural = lax.broadcasted_iota(jnp.int32, (per, chunk), 1)
        here = natural == j * groups + me
        return jnp.concatenate(
            [jnp.sum(jnp.where(here, s2buf[source, k:k + 1, :], 0.0), axis=1, keepdims=True)
             for k in range(lines)], axis=0)

    def all_rows(q):
        def step(u, carry):
            at = [source_rows(u, n) for n in range(4)]
            a = [held[q, at[n], :].astype(F32) for n in range(4)]
            one = [(a[0] + a[2]) * inv_root, (a[1] + a[3]) * inv_root,
                   (a[0] - a[2]) * inv_root, (a[1] - a[3]) * inv_root]
            b = [(second_scale(u + n * quarter) * one[n]).astype(BF16).astype(F32)
                 for n in range(4)]
            held[q, at[0], :] = ((b[0] + b[1]) * inv_root).astype(BF16)
            held[q, at[1], :] = ((b[0] - b[1]) * inv_root).astype(BF16)
            held[q, at[2], :] = ((b[2] + b[3]) * inv_root).astype(BF16)
            held[q, at[3], :] = ((b[2] - b[3]) * inv_root).astype(BF16)
            return carry

        lax.fori_loop(0, quarter, step, 0)

    def chain(q, chip, way):
        e = 2 * chip + core
        to = (me + 2) % groups if way == 0 else (me + groups - 2) % groups
        return remote(tops.at[q, e], tops.at[q, e], chain_send.at[q, way, chip],
                      top_recv.at[q, e], row=to)

    def to_core(q, e):
        return remote(tops.at[q, e], tops.at[q, e], core_send.at[q, e], top_recv.at[q, e],
                      row=sibling)

    def to_x(q, e):
        return remote(tops.at[q, e, :, 1 - x], tops_x.at[q, e], x_send.at[q, e], x_recv.at[q, e],
                      col=col_x)

    def to_y(q, e):
        return remote(tops.at[q, e, 1 - y], tops_y.at[q, e], y_send.at[q, e], y_recv.at[q, e],
                      col=col_y)

    def x_core(q, e):
        return remote(tops_x.at[q, e], tops_x.at[q, e], xc_send.at[q, e], x_recv.at[q, e],
                      row=sibling)

    def y_core(q, e):
        return remote(tops_y.at[q, e], tops_y.at[q, e], yc_send.at[q, e], y_recv.at[q, e],
                      row=sibling)

    def spread(q, chip):
        e = 2 * chip + core
        to_x(q, e).start()
        to_y(q, e).start()
        to_core(q, e).start()

    def begin(q):
        @pl.when(z + 1 < chips)
        def _():
            chain(q, z, 0).start()

        @pl.when(z > 0)
        def _():
            chain(q, z, 1).start()

        spread(q, z)

    def onward(q, k):
        @pl.when(z >= k)
        def _():
            chain(q, z - k, 0).wait_recv()

            @pl.when(z + 1 < chips)
            def _():
                chain(q, z - k, 0).start()

            spread(q, z - k)

        @pl.when(z + k < chips)
        def _():
            chain(q, z + k, 1).wait_recv()

            @pl.when(z > 0)
            def _():
                chain(q, z + k, 1).start()

            spread(q, z + k)

    def collect(q):
        for chip in range(chips):
            e = 2 * chip + core
            to_x(q, e).wait_recv()
            x_core(q, e).start()
            to_y(q, e).wait_recv()
            y_core(q, e).start()
        for chip in range(chips):
            other = 2 * chip + 1 - core
            to_core(q, other).wait_recv()
            x_core(q, other).wait_recv()
            y_core(q, other).wait_recv()

    pieces = [(e, slice(n * per, (n + 1) * per))
              for n in range(block_rows // per) for e in range(groups)]

    def own_top(q, by, bx):
        return jnp.concatenate([tops[q, e, by, bx, at, :] for e, at in pieces], axis=0)

    def far_top(ref, q, b):
        return jnp.concatenate([ref[q, e, b, at, :] for e, at in pieces], axis=0)

    tile = 256
    tiles = half // tile

    def product(a, b):
        return jnp.dot(a, b, preferred_element_type=F32)

    def sum_copy(q, t, high):
        at = pl.ds(t * tile + (half if high else 0), tile)
        n = t + (tiles if high else 0)
        return remote(part_out.at[q, at], part_in.at[q, at], sum_send.at[q, n], sum_recv.at[q, n],
                      col=col_x if high else col_y)

    def send_sums(q):
        def step(t, carry):
            at, upper = pl.ds(t * tile, tile), pl.ds(half + t * tile, tile)
            part_out[q, at, :] = (product(own[at, :], far_top(tops_y, q, x)) +
                                  product(near_x[at, :], far_top(tops_y, q, 1 - x))).astype(BF16)
            sum_copy(q, t, False).start()
            part_out[q, upper, :] = (product(own[upper, :], far_top(tops_x, q, y)) +
                                     product(near_y[at, :], far_top(tops_x, q, 1 - y))
                                     ).astype(BF16)
            sum_copy(q, t, True).start()
            return carry

        lax.fori_loop(0, tiles, step, 0)

    def own_sums(q):
        def step(t, carry):
            at, upper = pl.ds(t * tile, tile), pl.ds(half + t * tile, tile)
            mine = own_top(q, y, x)
            total[q, at, :] = held[q, at, :].astype(F32) - (
                product(own[at, :], mine) + product(near_x[at, :], own_top(q, y, 1 - x)))
            total[q, upper, :] = held[q, upper, :].astype(F32) - (
                product(own[upper, :], mine) + product(near_y[at, :], own_top(q, 1 - y, x)))
            return carry

        lax.fori_loop(0, tiles, step, 0)

    def finish(q):
        lanes = slice(q * width, (q + 1) * width)

        def step(t, carry):
            for high in (False, True):
                sum_copy(q, t, high).wait_recv()
                at = pl.ds(t * tile + (half if high else 0), tile)
                out[at, lanes] = (total[q, at, :] - part_in[q, at, :].astype(F32)).astype(BF16)
            return carry

        lax.fori_loop(0, tiles, step, 0)

    top_rows(0)
    begin(0)
    all_rows(0)
    onward(0, 1)
    exchange(1)
    panel_x.wait_recv()
    panel_y.wait_recv()
    regroup(near_x)
    regroup(near_y)
    onward(0, 2)
    top_rows(1)
    begin(1)
    all_rows(1)
    onward(0, 3)
    onward(1, 1)
    collect(0)
    onward(1, 2)
    send_sums(0)
    onward(1, 3)
    collect(1)
    send_sums(1)
    own_sums(0)
    finish(0)
    own_sums(1)
    finish(1)

    for copy in sends + [panel_x, panel_y]:
        copy.wait_send()
    for q in range(parts):
        for chip in range(chips):
            @pl.when((z + 1 < chips) & (chip <= z))
            def _():
                chain(q, chip, 0).wait_send()

            @pl.when((z > 0) & (chip >= z))
            def _():
                chain(q, chip, 1).wait_send()

            e = 2 * chip + core
            for copy in (to_x(q, e), to_y(q, e), to_core(q, e), x_core(q, e), y_core(q, e)):
                copy.wait_send()

        def done(t, carry):
            sum_copy(q, t, False).wait_send()
            sum_copy(q, t, True).wait_send()
            return carry

        lax.fori_loop(0, tiles, done, 0)


def paired_scratch(groups, parts, rows, block, width):
    dma = pltpu.SemaphoreType.DMA
    piece, upper = width // parts, block // groups
    pair = dma((parts, groups))
    return [
        pltpu.VMEM((parts, groups, rows // groups, piece), BF16),
        pltpu.VMEM((parts, rows, piece), BF16),
        pltpu.VMEM((groups, rows // 256, 256), F32),
        pltpu.VMEM((parts, groups, 2, 2, upper, piece), BF16),
        pltpu.VMEM((parts, groups, 2, upper, piece), BF16),
        pltpu.VMEM((parts, groups, 2, upper, piece), BF16),
        pltpu.VMEM((rows, block), BF16),
        pltpu.VMEM((rows // 2, block), BF16),
        pltpu.VMEM((rows // 2, block), BF16),
        pltpu.VMEM((parts, rows, piece), BF16),
        pltpu.VMEM((parts, rows, piece), BF16),
        pltpu.VMEM((parts, rows, piece), F32),
        dma((2 + parts,)), pair, pair, dma((groups,)), dma((groups,)), pair,
        dma((parts, 2, groups // 2)), pair,
        pair, pair, pair, pair, pair, pair,
        dma((parts, rows // 256)), dma((parts, rows // 256)), dma((2,)), dma((2,)),
    ]


def per_device(slab_block, scale_first, scale_second, panel_lower):
    rows, width = slab_block.shape
    block = panel_lower.shape[1]
    groups, cols = lax.axis_size("row"), lax.axis_size("col")
    per_source = rows // groups
    top = cols * block // groups
    chunk = max(256, 16 * groups)
    vmem = pl.BlockSpec(memory_space=pltpu.VMEM)
    dma = pltpu.SemaphoreType.DMA
    if groups == 8 and cols == 4 and rows == 2 * block and width % 256 == 0:
        parts = 2
        run = functools.partial(paired_kernel, groups, parts)
        both = jnp.concatenate([scale_first, scale_second]).astype(F32)
        scales = [both.reshape(2 * rows // chunk, chunk)]
        scratch = paired_scratch(groups, parts, rows, block, width)
    else:
        run = functools.partial(kernel, groups, cols)
        scales = [scale_first.astype(F32).reshape(rows // chunk, chunk),
                  scale_second.astype(F32).reshape(per_source, groups).T]
        scratch = [
            pltpu.VMEM((groups, per_source, width), BF16),
            pltpu.VMEM((rows, width), BF16),
            pltpu.VMEM((groups, groups, per_source), F32),
            pltpu.VMEM((groups, top, width), BF16),
            pltpu.VMEM((cols * block, width), BF16),
            pltpu.VMEM((rows, width), F32),
            pltpu.VMEM((cols, rows, block), BF16),
            dma((4,)),
            dma((groups,)), dma((groups,)), dma((groups,)), dma((groups,)),
            dma((groups,)), dma((groups,)), dma((groups,)),
            dma((max(6, cols),)), dma((max(6, cols),)),
        ]
    return pl.pallas_call(
        run,
        out_shape=jax.ShapeDtypeStruct((rows, width), BF16),
        in_specs=[vmem] * (1 + len(scales)) + [pl.BlockSpec(memory_space=pl.ANY)],
        out_specs=vmem,
        scratch_shapes=scratch,
        compiler_params=pltpu.CompilerParams(
            collective_id=0, has_side_effects=True, vmem_limit_bytes=56 * 2**20),
        cost_estimate=pl.CostEstimate(
            flops=2 * rows * cols * block * width,
            bytes_accessed=2 * (rows * width * 2 + rows * block), transcendentals=0),
    )(slab_block, *scales, panel_lower)


def solution(mesh):
    placed = (P("row", "col"), P("row"), P("row"), P("row", "col"))
    return jax.shard_map(
        per_device, mesh=mesh, in_specs=placed, out_specs=P("row", "col"), check_vma=False
    )
```
